32 devices in a mesh: dp: 4 (over y, x), expert: 8 (over z, core).
Axes of the slice: x: 2, y: 2, z: 4, core: 2. Of those that a mesh axis runs over, the one named last changes fastest.
Arguments:
- route_ids: int32 [4096, 8], P(('dp', 'expert')), may hold values from 0 to 15, all different within a row; in each aligned block of 1024 rows (0 to 1023, 1024 to 2047, ...) at most 640 rows name the same one
- counts: int32 [4096], P(('dp', 'expert')), may hold values from 1 to 8
- slot_probs: bfloat16 [4096, 8], P(('dp', 'expert')), may hold values from 0.019897461 to 0.5
- cotangent: bfloat16 [4096, 2048], P(('dp', 'expert')), may hold values from -0.9 to 0.9
- saved_hidden: bfloat16 [4, 16, 640, 768], P('dp', 'expert'), may hold values from -4.6 to 4.6
- down_weight: bfloat16 [16, 768, 2048], P('expert'), may hold values from -0.21875 to 0.21875
Outputs:
- router_grad: float32 [4096, 8], P(('dp', 'expert'))
- merged_grad: float32 [16, 768, 2048], P('expert', 'dp')
The draws below stay inside these ranges and needn't reach their ends.
Inputs may be any that keep to these rules, and one draw needn't show every extreme that they name: `route_ids`: each token names 8 different experts; only its first counts slots are its support; among the 1024 tokens of one replica no expert is named by more than 640 tokens.
All inputs are finite; a program needn't handle non-finite values.
Results may differ from the reference program's by a relative error of at most 0.0011.
Values may be sent and summed in bfloat16 or wider, within the bound.
A program may use at most 128 MiB of HBM per device.

```python
import math
import jax
import jax.numpy as jnp
import numpy as np
from jax import lax

D = 2048
FF = 768
TOPK = 8
EXPERTS = 16
ROWS = 1024
CAP = 640
TOKENS = 4096
N_DP = 4


def draw_cotangent(key, part):
    key = jax.random.fold_in(key, 11)
    key_dir, key_noise = jax.random.split(key, 2)
    direction = jax.random.truncated_normal(key_dir, -3.0, 3.0, (D,), jnp.float32)
    noise = jax.random.truncated_normal(key_noise, -4.0, 4.0, (TOKENS, D), jnp.float32)
    return (0.05 * (0.6 * direction + noise)).astype(jnp.bfloat16)


def draw_saved_hidden(key, part):
    key = jax.random.fold_in(key, 23)
    key_mean, key_noise = jax.random.split(key, 2)
    shape = (N_DP, EXPERTS, CAP, FF)
    center = jax.random.uniform(key_mean, (FF,), jnp.float32, 0.0, 0.6)
    noise = jax.random.truncated_normal(key_noise, -4.0, 4.0, shape, jnp.float32)
    return (center + noise).astype(jnp.bfloat16)


def set_ends(array, rng, smallest, largest):
    index_at = [jax.random.randint(jax.random.fold_in(rng, axis), (), 0, length) for axis, length in enumerate(array.shape)]
    main_axis = array.shape.index(max(array.shape))
    neighbour = index_at[:main_axis] + [(index_at[main_axis] + 1) % array.shape[main_axis]] + index_at[main_axis + 1:]
    return array.at[tuple(index_at)].set(smallest).at[tuple(neighbour)].set(largest)


def level_of(stream_key, extent, cuts, least, largest):
    factor_of = 1.0
    for axis_at, shards_of in cuts:
        steps = jax.random.uniform(jax.random.fold_in(jax.random.fold_in(stream_key, 6), axis_at), (shards_of,), jnp.float32, least / len(cuts), largest / len(cuts))
        factor_of = factor_of * jnp.repeat(jnp.exp(steps), extent[axis_at] // shards_of).reshape((-1,) + (1,) * (len(extent) - 1 - axis_at))
    return factor_of


def assign_block(rng, own, number, rows, amount, top, most, slope):
    order = jax.random.permutation(rng, amount)
    crowded, ordinary = portions_of(amount, rows * top, most, slope, True), portions_of(amount, rows * top, most, slope, False)
    places = jnp.arange(amount)

    def named(lengths, rotation):
        used = int((lengths > 0).sum())
        fixed = max(1, used // 4)
        moved = fixed + (places - fixed + rotation * (used - fixed)) % max(1, amount - fixed)
        return jnp.zeros((amount,), jnp.int32).at[order[jnp.where(places < fixed, places, moved)]].set(jnp.asarray(lengths, jnp.int32))

    lengths = jnp.where(number % 4 == 0, named(crowded, number // 4), named(ordinary, number - number // 4 - 1))
    mixed = jax.random.permutation(jax.random.fold_in(own, 3), amount)
    source_of, sink = mixed[0:amount // 2 * 2:2], mixed[1:amount // 2 * 2:2]
    slack = jnp.minimum(lengths[source_of] - 1, most - lengths[sink]) // 2
    slack = jnp.where((source_of == order[0]) | (sink == order[0]) | (lengths[sink] == 0), 0, jnp.maximum(slack, 0))
    moved = jax.random.randint(jax.random.fold_in(own, 4), (amount // 2,), 0, 1 << 20) % (slack + 1)
    lengths = lengths.at[source_of].add(-moved).at[sink].add(moved)
    labels = jnp.searchsorted(jnp.cumsum(lengths), jnp.arange(rows * top), side="right").astype(jnp.int32)
    table = labels.reshape(top, rows).T
    table = table[jax.random.permutation(jax.random.fold_in(own, 1), rows)]
    rotation = jax.random.randint(jax.random.fold_in(own, 2), (rows, 1), 0, top)
    return jnp.take_along_axis(table, (jnp.arange(top)[None, :] + rotation) % top, axis=1)


def portions_of(number_of, total, limit, skew, full):
    loads = [(1 << 20) // math.isqrt(standing ** skew) + 1 for standing in range(1, number_of + 1)]
    largest = limit if full else min(limit, max(-(-total // number_of), total * loads[0] // sum(loads)))
    least = 1 if total - largest >= number_of - 1 else 0
    given, surplus = [largest] + [least] * (number_of - 1), total - largest - least * (number_of - 1)
    while surplus > 0:
        free = [i for i in range(1, number_of) if given[i] < largest] or [i for i in range(1, number_of) if given[i] < limit]
        mass, left = sum([loads[i] for i in free]), surplus
        for i in free:
            extra = min(limit - given[i], max(1, left * loads[i] // mass), surplus)
            given[i] = given[i] + extra
            surplus = surplus - extra
    return np.array(given)


def bell_draw(key, extent, scale, reach, pieces=(), kind=jnp.bfloat16):
    entries = scale * jax.random.normal(key, extent, jnp.float32)
    if pieces:
        entries = entries * level_of(key, extent, pieces, -0.22, 0.18)
    return jnp.clip(entries, -reach, reach).astype(kind)


def setup_inputs(seed: int = 0) -> dict:
    key_list = jax.random.split(jax.random.key(seed), 7)
    route_ids_keys = jax.random.split(jax.random.fold_in(key_list[0], 1), TOKENS // ROWS)
    route_ids_turns = jax.random.permutation(jax.random.fold_in(key_list[0], 3), TOKENS // ROWS)
    route_ids = jax.vmap(lambda own, number: assign_block(jax.random.fold_in(key_list[0], 2), own, number, ROWS, EXPERTS, TOPK, CAP, 2))(route_ids_keys, route_ids_turns).reshape((TOKENS, TOPK))
    counts = set_ends(jax.random.randint(key_list[1], (TOKENS,), 1, TOPK + 1), jax.random.fold_in(key_list[1], 1), 1, TOPK).astype(jnp.int32)
    slot_probs = jnp.clip(jnp.exp(math.log(0.5) - 3.224016 * jax.random.uniform(key_list[2], (TOKENS, TOPK), jnp.float32) ** level_of(key_list[2], (TOKENS, TOPK), ((0, 32),), -0.2, 0.2)), 0.019897461, 0.5).astype(jnp.bfloat16)
    cotangent = draw_cotangent(jax.random.fold_in(key_list[6], 71), 0)
    saved_hidden = draw_saved_hidden(jax.random.fold_in(key_list[6], 71), 0)
    down_weight = bell_draw(key_list[5], (EXPERTS, FF, D), FF ** -0.5, 0.21875, ((0, 8),))
    return {"route_ids": route_ids, "counts": counts, "slot_probs": slot_probs, "cotangent": cotangent, "saved_hidden": saved_hidden, "down_weight": down_weight}


epsilon = 1e-6


def adasum_pair(left_grad, right_grad):
    inner = jnp.sum(left_grad * right_grad, axis=-1, keepdims=True)
    left_norm = jnp.sum(left_grad * left_grad, axis=-1, keepdims=True)
    right_norm = jnp.sum(right_grad * right_grad, axis=-1, keepdims=True)
    left_coef = 1.0 - inner / (2.0 * (left_norm + epsilon))
    right_coef = 1.0 - inner / (2.0 * (right_norm + epsilon))
    return left_coef * left_grad + right_coef * right_grad


def pick_rows(rows, index):
    return rows[index]


def reference(route_ids, counts, slot_probs, cotangent, saved_hidden, down_weight):
    slot_index = jnp.arange(TOPK, dtype=jnp.int32)
    live_slots = slot_index[None, :] < counts[:, None]
    gate_probs = jnp.where(live_slots, slot_probs.astype(jnp.float32), 0.0)
    onehot = route_ids[:, :, None] == jnp.arange(EXPERTS, dtype=jnp.int32)[None, None, :]
    gate = jnp.sum(jnp.where(onehot, gate_probs[:, :, None], 0.0), axis=1)
    live_hits = jnp.sum(jnp.where(onehot & live_slots[:, :, None], 1, 0), axis=1).astype(jnp.int32)
    cotangents = cotangent.astype(jnp.float32).reshape(N_DP, ROWS, D)
    padded_cot = jnp.concatenate([cotangents, jnp.zeros((N_DP, 1, D), jnp.float32)], axis=1)
    gate_rows = gate.reshape(N_DP, ROWS, EXPERTS)
    hit_rows = live_hits.reshape(N_DP, ROWS, EXPERTS)
    level_count = N_DP.bit_length() - 1
    replica_index = jnp.arange(N_DP, dtype=jnp.int32)[:, None]
    row_index = jnp.broadcast_to(jnp.arange(ROWS, dtype=jnp.int32)[None, :], (N_DP, ROWS))

    def one_expert(expert):
        hit = lax.dynamic_index_in_dim(hit_rows, expert, 2, keepdims=False)
        column = lax.dynamic_index_in_dim(gate_rows, expert, 2, keepdims=False)
        places = (jnp.cumsum(hit, axis=1) - 1).astype(jnp.int32)
        target = jnp.where(hit > 0, places, CAP).astype(jnp.int32)
        token_of_slot = jnp.full((N_DP, CAP + 1), ROWS, jnp.int32).at[replica_index, target].set(row_index)
        token_of_slot = token_of_slot[:, :CAP]
        slot_cot = jax.vmap(pick_rows)(padded_cot, token_of_slot)
        padded_gate = jnp.concatenate([column, jnp.zeros((N_DP, 1), jnp.float32)], axis=1)
        slot_gate = jax.vmap(pick_rows)(padded_gate, token_of_slot)
        hidden = lax.dynamic_index_in_dim(saved_hidden, expert, 1, keepdims=False).astype(jnp.float32)
        scaled = (slot_gate[:, :, None] * slot_cot).astype(jnp.bfloat16)
        scaled = lax.optimization_barrier(scaled).astype(jnp.float32)
        grad_rows = jnp.einsum("rcf,rcd->rfd", hidden, scaled, precision=lax.Precision.HIGHEST)
        weight = lax.dynamic_index_in_dim(down_weight, expert, 0, keepdims=False).astype(jnp.float32)
        outputs = jnp.einsum("rcf,fd->rcd", hidden, weight, precision=lax.Precision.HIGHEST)
        slot_scores = jnp.sum(outputs * slot_cot, axis=-1)
        safe_places = jnp.clip(places, 0, CAP - 1).astype(jnp.int32)
        scores = jnp.where(hit > 0, jnp.take_along_axis(slot_scores, safe_places, axis=1), 0.0)
        merged = grad_rows
        for level_index in range(level_count):
            half_rows = merged.shape[0] // 2
            merged = adasum_pair(merged[:half_rows], merged[half_rows:])
        return merged[0], scores.reshape(TOKENS)

    merged_grad, scores = lax.map(one_expert, jnp.arange(EXPERTS, dtype=jnp.int32))
    picked = jnp.sum(jnp.where(onehot, scores.T[:, None, :], 0.0), axis=2)
    average = jnp.sum(jnp.where(live_slots, picked, 0.0), axis=1) / counts.astype(jnp.float32)
    router_grad = jnp.where(live_slots, picked - average[:, None], 0.0)
    return router_grad, merged_grad
```

```python
import functools

import jax
import jax.numpy as jnp
from jax import lax
from jax.experimental import pallas as pl
from jax.experimental.pallas import tpu as pltpu
from jax.sharding import PartitionSpec as P

epsilon = 1e-06


def carried_in(value, axis, join, neutral):
    count, mine = (lax.axis_size(axis), lax.axis_index(axis))
    pieces = lax.all_gather(value, axis)
    running = jnp.full_like(value, 0) + jnp.asarray(neutral, value.dtype)

    def lap(position, running):
        longer = join(running, pieces[position])
        return jnp.where(position < mine, longer, running)

    return lax.fori_loop(0, count - 1, lap, running)


def adasum_pair(left_grad, right_grad):
    inner = jnp.sum(left_grad * right_grad, axis=-1, keepdims=True)
    left_norm = jnp.sum(left_grad * left_grad, axis=-1, keepdims=True)
    right_norm = jnp.sum(right_grad * right_grad, axis=-1, keepdims=True)
    left_coef = 1.0 - inner / (2.0 * (left_norm + epsilon))
    right_coef = 1.0 - inner / (2.0 * (right_norm + epsilon))
    return left_coef * left_grad + right_coef * right_grad


def add_counts(earlier, later):
    return earlier + later


def local(route_ids, counts, slot_probs, cotangent, saved_hidden, down_weight):
    token_count = cotangent.shape[0]
    model_width = cotangent.shape[1]
    slot_count = route_ids.shape[1]
    owners = lax.axis_size("expert")
    local_count = down_weight.shape[0]
    hidden_width = down_weight.shape[1]
    experts = local_count * owners
    slot_index = jnp.arange(slot_count, dtype=jnp.int32)
    live_slots = slot_index[None, :] < counts[:, None]
    gate_probs = jnp.where(live_slots, slot_probs.astype(jnp.float32), 0.0)
    onehot = route_ids[:, :, None] == jnp.arange(experts, dtype=jnp.int32)[None, None, :]
    weights = jnp.sum(jnp.where(onehot, gate_probs[:, :, None], 0.0), axis=1).astype(jnp.bfloat16)
    live_hits = jnp.sum(jnp.where(onehot & live_slots[:, :, None], 1, 0), axis=1).astype(jnp.int32)
    local_counts = jnp.sum(live_hits, axis=0)
    offsets = carried_in(local_counts, "expert", add_counts, jnp.zeros_like(local_counts))
    running = jnp.cumsum(live_hits, axis=0) - 1 + offsets[None, :]
    token_places = jnp.where(live_hits > 0, running, -1).astype(jnp.int32)
    first_expert = lax.axis_index("expert") * local_count
    hidden = saved_hidden[0]
    capacity = hidden.shape[1]
    row_count = token_count * owners
    slot_iota = jnp.arange(capacity, dtype=jnp.int32)
    positions = jnp.full((local_count, row_count), -1, jnp.int32)
    cotangents = lax.all_gather(cotangent, "expert", axis=0, tiled=True)
    gate_rows = lax.all_gather(weights, "expert", axis=0, tiled=True)
    place_rows = lax.all_gather(token_places, "expert", axis=0, tiled=True)
    columns = lax.dynamic_slice_in_dim(gate_rows, first_expert, local_count, 1)
    places = lax.dynamic_slice_in_dim(place_rows, first_expert, local_count, 1)
    select = (places.T[:, None, :] == slot_iota[None, :, None]).astype(jnp.bfloat16)
    slot_rows = jnp.einsum(
        "ecn,nd->ecd", select, cotangents, preferred_element_type=jnp.float32
    ).astype(jnp.bfloat16)
    slot_gates = jnp.einsum("ecn,ne->ec", select, columns, preferred_element_type=jnp.float32)
    positions = lax.dynamic_update_slice_in_dim(positions, places.T, jnp.int32(0), 1)
    slot_rows, slot_gates, positions = (slot_rows, slot_gates, positions)
    wide_rows = slot_rows.astype(jnp.float32)
    scaled = (slot_gates[:, :, None] * wide_rows).astype(jnp.bfloat16)
    grad_rows = jnp.einsum("ecf,ecd->efd", hidden, scaled, preferred_element_type=jnp.float32)
    outputs = jnp.einsum("ecf,efd->ecd", hidden, down_weight, preferred_element_type=jnp.float32)
    slot_scores = jnp.sum(outputs * wide_rows, axis=-1)
    safe_places = jnp.maximum(positions, 0)
    scores = jnp.where(positions >= 0, jnp.take_along_axis(slot_scores, safe_places, axis=1), 0.0)
    returned = lax.all_to_all(
        scores.reshape(local_count, owners, token_count),
        "expert",
        split_axis=1,
        concat_axis=0,
        tiled=True,
    )
    returned = returned.reshape(experts, token_count)
    picked = jnp.sum(jnp.where(onehot, returned.T[:, None, :], 0.0), axis=2)
    average = jnp.sum(jnp.where(live_slots, picked, 0.0), axis=1) / counts.astype(jnp.float32)
    router_grad = jnp.where(live_slots, picked - average[:, None], 0.0)
    replicas = lax.axis_size("dp")
    level_count = replicas.bit_length() - 1
    shard_rows = hidden_width // replicas
    stacked = lax.all_to_all(
        grad_rows.reshape(local_count, replicas, shard_rows, model_width),
        "dp",
        split_axis=1,
        concat_axis=1,
        tiled=True,
    )
    for level_index in range(level_count):
        half_rows = stacked.shape[1] // 2
        stacked = adasum_pair(stacked[:, :half_rows], stacked[:, half_rows:])
    merged = stacked[:, 0]
    return (router_grad, merged)


MESH = pl.DeviceIdType.MESH
CHUNKS = 4
TOP = 32767.0


def flipped(position, mask):
    result = position
    bit = 1
    while bit <= mask:
        if mask & bit:
            result = result + bit * (1 - 2 * ((position // bit) % 2))
        bit *= 2
    return result


def merge_kernel(
    owners, replicas, chunks,
    gates_ref, cot_ref, hid_ref, w_ref,
    score_ref, out_ref,
    cots, gates, hid, weight, hid_t, tok_t, gate_cols, scaled, own, enc, enc_scale, got, got_scale, score_mine, score_back,
    load_sem, own_sem, gate_s, gate_r, direct_s, direct_r, forward_s, forward_r,
    grad_s, grad_r, scale_s, scale_r, back_s, back_r,
):
    me = lax.axis_index("expert")
    mine = lax.axis_index("dp")
    sibling = me + 1 - 2 * (me % 2)
    pairs = owners // 2
    tokens = cot_ref.shape[0]
    width = cot_ref.shape[1] // chunks
    local_count, capacity, hidden_width = hid.shape
    shard = hidden_width // replicas
    row_count = owners * tokens
    lanes = got_scale.shape[-1]

    barrier = pltpu.get_barrier_semaphore()
    for j in range(1, owners):
        pl.semaphore_signal(barrier, inc=1, device_id={"expert": (me + j) % owners}, device_id_type=MESH)
    for m in range(1, replicas):
        pl.semaphore_signal(barrier, inc=1, device_id={"dp": flipped(mine, m)}, device_id_type=MESH)

    load_hid = pltpu.make_async_copy(hid_ref, hid, load_sem.at[0])
    load_w = pltpu.make_async_copy(w_ref, weight, load_sem.at[1])

    def block(source):
        return pl.ds(pl.multiple_of(source * tokens, tokens), tokens)

    def columns(k):
        return pl.ds(pl.multiple_of(k * width, width), width)

    def own_copy(k):
        return pltpu.make_async_copy(cot_ref.at[:, columns(k)], cots.at[k, block(me)], own_sem.at[k])

    def gate_copy(j):
        target = (me + j) % owners
        return pltpu.make_async_remote_copy(
            gates_ref.at[target], gates.at[me], gate_s.at[j - 1], gate_r.at[j - 1],
            device_id={"expert": target}, device_id_type=MESH)

    def direct_copy(j, k):
        target = sibling if j == 0 else (me + 2 * j) % owners
        return pltpu.make_async_remote_copy(
            cot_ref.at[:, columns(k)], cots.at[k, block(me)], direct_s.at[j, k], direct_r.at[j, k],
            device_id={"expert": target}, device_id_type=MESH)

    def forward_copy(j, k):
        piece = cots.at[k, block((me + owners - 2 * j) % owners)]
        return pltpu.make_async_remote_copy(
            piece, piece, forward_s.at[j - 1, k], forward_r.at[j - 1, k],
            device_id={"expert": sibling}, device_id_type=MESH)

    def grad_copy(m, k):
        return pltpu.make_async_remote_copy(
            enc.at[m - 1, k], got.at[m - 1, k], grad_s.at[m - 1, k], grad_r.at[m - 1, k],
            device_id={"dp": flipped(mine, m)}, device_id_type=MESH)

    def scale_copy(m, k):
        return pltpu.make_async_remote_copy(
            enc_scale.at[m - 1, k], got_scale.at[m - 1, k], scale_s.at[m - 1, k], scale_r.at[m - 1, k],
            device_id={"dp": flipped(mine, m)}, device_id_type=MESH)

    def back_copy(j):
        target = (me + j) % owners
        return pltpu.make_async_remote_copy(
            score_mine.at[target], score_back.at[me], back_s.at[j - 1], back_r.at[j - 1],
            device_id={"expert": target}, device_id_type=MESH)

    load_hid.start()
    pl.semaphore_wait(barrier, owners - 1 + replicas - 1)
    for j in range(1, owners):
        gate_copy(j).start()

    def send_cots(k):
        for j in range(pairs):
            direct_copy(j, k).start()

    send_cots(0)

    def start_own(k, carry):
        own_copy(k).start()
        return carry

    lax.fori_loop(0, chunks, start_own, 0)
    load_w.start()
    gates[me] = gates_ref[me]
    score_mine[...] = jnp.zeros_like(score_mine)
    enc_scale[...] = jnp.zeros_like(enc_scale)

    load_hid.wait()

    def turn(b, carry):
        rows = pl.ds(pl.multiple_of(b * 128, 128), 128)
        for e in range(local_count):
            hid_t[e, :, rows] = hid[e, rows, :].astype(jnp.float32).T.astype(jnp.bfloat16)
        return carry

    lax.fori_loop(0, capacity // 128, turn, 0)

    for j in range(1, owners):
        gate_copy(j).wait_recv()

    eye = (lax.broadcasted_iota(jnp.int32, (tokens, tokens), 0)
           == lax.broadcasted_iota(jnp.int32, (tokens, tokens), 1))
    upper = (lax.broadcasted_iota(jnp.int32, (tokens, tokens), 0)
             <= lax.broadcasted_iota(jnp.int32, (tokens, tokens), 1)).astype(jnp.bfloat16)
    slots = lax.broadcasted_iota(jnp.int32, (capacity, 2 * tokens), 0)
    for e in range(local_count):
        rows = jnp.concatenate([gates[s, e:e + 1, :] for s in range(owners)], axis=0)
        hit = rows > 0.0
        inside = jnp.dot(jnp.where(hit, 1.0, 0.0).astype(jnp.bfloat16), upper, preferred_element_type=jnp.float32)
        before = jnp.zeros((1, 1), jnp.float32)
        places = []
        for s in range(owners):
            place = inside[s:s + 1, :] + before - 1.0
            places.append(jnp.where(hit[s:s + 1, :], place, -1.0).astype(jnp.int32))
            before = before + inside[s:s + 1, tokens - 1:tokens]
            column = jnp.sum(jnp.where(eye, rows[s:s + 1, :], 0.0), axis=1, keepdims=True)
            gate_cols[e, s * tokens:(s + 1) * tokens, :] = jnp.broadcast_to(column, (tokens, 128))
        for pair in range(pairs):
            place = jnp.concatenate(places[2 * pair:2 * pair + 2], axis=1)
            select = jnp.where(slots == place, 1.0, 0.0).astype(jnp.bfloat16)
            tok_t[e, :, pair * 2 * tokens:(pair + 1) * 2 * tokens] = jnp.dot(
                hid_t[e], select, preferred_element_type=jnp.float32).astype(jnp.bfloat16)

    mark = (lax.broadcasted_iota(jnp.int32, (shard, lanes), 0)
            == lax.broadcasted_iota(jnp.int32, (shard, lanes), 1))

    def step(k, carry):
        own_copy(k).wait()
        for j in range(1, pairs):
            direct_copy(j, k).wait_recv()
            forward_copy(j, k).start()
        direct_copy(0, k).wait_recv()

        @pl.when(k + 1 < chunks)
        def _():
            send_cots(k + 1)

        for j in range(1, pairs):
            forward_copy(j, k).wait_recv()

        def scale_block(s, carry):
            for e in range(local_count):
                gate = gate_cols[e, block(s), :]
                for c in range(width // 128):
                    part = cots[k, block(s), c * 128:(c + 1) * 128].astype(jnp.float32)
                    scaled[e, block(s), c * 128:(c + 1) * 128] = (gate * part).astype(jnp.bfloat16)
            return carry

        lax.fori_loop(0, owners, scale_block, 0)
        for m in list(range(replicas - 1, 0, -1)) + [0]:
            target = flipped(mine, m)
            rows = pl.ds(pl.multiple_of(target * shard, shard), shard)
            for e in range(local_count):
                grad = jnp.dot(tok_t[e, rows, :], scaled[e], preferred_element_type=jnp.float32)
                if m == 0:
                    own[k, e] = grad
                else:
                    largest = jnp.max(jnp.abs(grad), axis=1, keepdims=True)
                    factor = jnp.where(largest > 1e-30, TOP / largest, 0.0)
                    enc[m - 1, k, e] = jnp.round(grad * factor).astype(jnp.int32).astype(jnp.int16)
                    enc_scale[m - 1, k, e:e + 1, :] = jnp.sum(
                        jnp.where(mark, largest * (1.0 / TOP), 0.0), axis=0, keepdims=True)
            if m:
                scale_copy(m, k).start()
                grad_copy(m, k).start()
        return carry

    lax.fori_loop(0, chunks, step, 0)

    load_w.wait()
    half = hidden_width // 256

    def score_pair(pair, carry):
        toks = pl.ds(pl.multiple_of(pair * 2 * tokens, 2 * tokens), 2 * tokens)
        for e in range(local_count):
            total = jnp.zeros((1, 2 * tokens), jnp.float32)
            for f in range(half):
                part = jnp.zeros((256, 2 * tokens), jnp.float32)
                for k in range(chunks):
                    part = part + lax.dot_general(
                        weight[e, f * 256:(f + 1) * 256, k * width:(k + 1) * width], cots[k, toks, :],
                        (((1,), (1,)), ((), ())), preferred_element_type=jnp.float32)
                total = total + jnp.sum(
                    part * tok_t[e, f * 256:(f + 1) * 256, toks].astype(jnp.float32), axis=0, keepdims=True)
            score_mine[2 * pair, e:e + 1, :] = total[:, :tokens]
            score_mine[2 * pair + 1, e:e + 1, :] = total[:, tokens:]
        return carry

    lax.fori_loop(0, pairs, score_pair, 0)
    for j in range(1, owners):
        back_copy(j).start()
    score_back[me] = score_mine[me]

    for k in range(chunks):
        for m in range(1, replicas):
            scale_copy(m, k).wait_recv()
            grad_copy(m, k).wait_recv()

    lane = lax.broadcasted_iota(jnp.int32, (16, lanes), 1)
    sublane = lax.broadcasted_iota(jnp.int32, (16, lanes), 0)

    def dots(left, right):
        return jnp.sum(sum(a * b for a, b in zip(left, right)), axis=1, keepdims=True)

    def merge_rows(b, carry):
        rows = pl.ds(pl.multiple_of(b * 16, 16), 16)
        here = lane == sublane + b * 16
        for e in range(local_count):
            grads = [[own[k, e, rows, :] for k in range(chunks)]]
            for m in range(1, replicas):
                parts = []
                for k in range(chunks):
                    scale = jnp.sum(jnp.where(here, got_scale[m - 1, k, e:e + 1, :], 0.0), axis=1, keepdims=True)
                    parts.append(got[m - 1, k, e, rows, :].astype(jnp.int32).astype(jnp.float32) * scale)
                grads.append(parts)
            while len(grads) > 1:
                count = len(grads) // 2
                merged = []
                for left, right in zip(grads[:count], grads[count:]):
                    inner = dots(left, right)
                    left_coef = 1.0 - inner / (2.0 * (dots(left, left) + epsilon))
                    right_coef = 1.0 - inner / (2.0 * (dots(right, right) + epsilon))
                    merged.append([left_coef * a + right_coef * b for a, b in zip(left, right)])
                grads = merged
            for k in range(chunks):
                out_ref[e, rows, k * width:(k + 1) * width] = grads[0][k]
        return carry

    lax.fori_loop(0, shard // 16, merge_rows, 0)

    for j in range(1, owners):
        back_copy(j).wait_recv()
    score_ref[...] = score_back[...]

    for j in range(1, owners):
        gate_copy(j).wait_send()
        back_copy(j).wait_send()

    def drain(k, carry):
        for j in range(pairs):
            direct_copy(j, k).wait_send()
            if j:
                forward_copy(j, k).wait_send()
        for m in range(1, replicas):
            scale_copy(m, k).wait_send()
            grad_copy(m, k).wait_send()
        return carry

    lax.fori_loop(0, chunks, drain, 0)


def fused(owners, replicas, route_ids, counts, slot_probs, cotangent, saved_hidden, down_weight):
    tokens, model_width = cotangent.shape
    slot_count = route_ids.shape[1]
    local_count, hidden_width = down_weight.shape[:2]
    capacity = saved_hidden.shape[2]
    experts = local_count * owners
    chunks = CHUNKS
    width = model_width // chunks
    shard = hidden_width // replicas
    lanes = -(-shard // 128) * 128
    others = replicas - 1
    pairs = owners // 2
    live_slots = jnp.arange(slot_count, dtype=jnp.int32)[None, :] < counts[:, None]
    onehot = route_ids[:, :, None] == jnp.arange(experts, dtype=jnp.int32)[None, None, :]
    gate_probs = jnp.where(live_slots, slot_probs.astype(jnp.float32), 0.0)
    weights = jnp.sum(jnp.where(onehot, gate_probs[:, :, None], 0.0), axis=1)
    gates = jnp.pad(weights.T.reshape(owners, local_count, tokens), ((0, 0), (0, 8 - local_count), (0, 0)))
    f32, bf16, i16 = jnp.float32, jnp.bfloat16, jnp.int16
    dma = pltpu.SemaphoreType.DMA
    vmem = pl.BlockSpec(memory_space=pltpu.VMEM)
    anywhere = pl.BlockSpec(memory_space=pl.ANY)
    scores, merged = pl.pallas_call(
        functools.partial(merge_kernel, owners, replicas, chunks),
        out_shape=(
            jax.ShapeDtypeStruct((owners, 8, tokens), f32),
            jax.ShapeDtypeStruct((local_count, shard, model_width), f32),
        ),
        in_specs=[vmem, anywhere, anywhere, anywhere],
        out_specs=(vmem, vmem),
        scratch_shapes=[
            pltpu.VMEM((chunks, owners * tokens, width), bf16),
            pltpu.VMEM((owners, 8, tokens), f32),
            pltpu.VMEM((local_count, capacity, hidden_width), bf16),
            pltpu.VMEM((local_count, hidden_width, model_width), bf16),
            pltpu.VMEM((local_count, hidden_width, capacity), bf16),
            pltpu.VMEM((local_count, hidden_width, owners * tokens), bf16),
            pltpu.VMEM((local_count, owners * tokens, 128), f32),
            pltpu.VMEM((local_count, owners * tokens, width), bf16),
            pltpu.VMEM((chunks, local_count, shard, width), f32),
            pltpu.VMEM((others, chunks, local_count, shard, width), i16),
            pltpu.VMEM((others, chunks, 8, lanes), f32),
            pltpu.VMEM((others, chunks, local_count, shard, width), i16),
            pltpu.VMEM((others, chunks, 8, lanes), f32),
            pltpu.VMEM((owners, 8, tokens), f32),
            pltpu.VMEM((owners, 8, tokens), f32),
            dma((2,)), dma((chunks,)),
            dma((owners - 1,)), dma((owners - 1,)),
            dma((pairs, chunks)), dma((pairs, chunks)),
            dma((pairs - 1, chunks)), dma((pairs - 1, chunks)),
            dma((others, chunks)), dma((others, chunks)),
            dma((others, chunks)), dma((others, chunks)),
            dma((owners - 1,)), dma((owners - 1,)),
        ],
        compiler_params=pltpu.CompilerParams(
            collective_id=0, has_side_effects=True, vmem_limit_bytes=56 * 2**20),
    )(gates, cotangent, saved_hidden[0], down_weight)
    returned = scores[:, :local_count].reshape(experts, tokens)
    picked = jnp.sum(jnp.where(onehot, returned.T[:, None, :], 0.0), axis=2)
    average = jnp.sum(jnp.where(live_slots, picked, 0.0), axis=1) / counts.astype(jnp.float32)
    router_grad = jnp.where(live_slots, picked - average[:, None], 0.0)
    return (router_grad, merged)


def chosen(owners, replicas, *arrays):
    cotangent, saved_hidden, down_weight = arrays[3:]
    local_count, hidden_width, model_width = down_weight.shape
    shard = hidden_width // replicas
    fits = (
        owners >= 4 and owners % 2 == 0 and local_count <= 8
        and replicas >= 2 and replicas & (replicas - 1) == 0 and shard % 16 == 0
        and hidden_width % 256 == 0 and model_width % (128 * CHUNKS) == 0
        and saved_hidden.shape[2] % 128 == 0 and cotangent.shape[0] == 128
    )
    return fused(owners, replicas, *arrays) if fits else local(*arrays)


def solution(mesh):
    in_specs = (
        P(("dp", "expert"), None),
        P(("dp", "expert")),
        P(("dp", "expert"), None),
        P(("dp", "expert"), None),
        P("dp", "expert", None, None),
        P("expert", None, None),
    )
    out_specs = (P(("dp", "expert"), None), P("expert", "dp", None))
    body = functools.partial(chosen, mesh.shape["expert"], mesh.shape["dp"])
    return jax.shard_map(body, mesh=mesh, in_specs=in_specs, out_specs=out_specs, check_vma=False)
```

```python
import functools

import jax
import jax.numpy as jnp
from jax import lax
from jax.experimental import pallas as pl
from jax.experimental.pallas import tpu as pltpu
from jax.sharding import PartitionSpec as P

epsilon = 1e-06


def carried_in(value, axis, join, neutral):
    count, mine = (lax.axis_size(axis), lax.axis_index(axis))
    pieces = lax.all_gather(value, axis)
    running = jnp.full_like(value, 0) + jnp.asarray(neutral, value.dtype)

    def lap(position, running):
        longer = join(running, pieces[position])
        return jnp.where(position < mine, longer, running)

    return lax.fori_loop(0, count - 1, lap, running)


def adasum_pair(left_grad, right_grad):
    inner = jnp.sum(left_grad * right_grad, axis=-1, keepdims=True)
    left_norm = jnp.sum(left_grad * left_grad, axis=-1, keepdims=True)
    right_norm = jnp.sum(right_grad * right_grad, axis=-1, keepdims=True)
    left_coef = 1.0 - inner / (2.0 * (left_norm + epsilon))
    right_coef = 1.0 - inner / (2.0 * (right_norm + epsilon))
    return left_coef * left_grad + right_coef * right_grad


def add_counts(earlier, later):
    return earlier + later


def local(route_ids, counts, slot_probs, cotangent, saved_hidden, down_weight):
    token_count = cotangent.shape[0]
    model_width = cotangent.shape[1]
    slot_count = route_ids.shape[1]
    owners = lax.axis_size("expert")
    local_count = down_weight.shape[0]
    hidden_width = down_weight.shape[1]
    experts = local_count * owners
    slot_index = jnp.arange(slot_count, dtype=jnp.int32)
    live_slots = slot_index[None, :] < counts[:, None]
    gate_probs = jnp.where(live_slots, slot_probs.astype(jnp.float32), 0.0)
    onehot = route_ids[:, :, None] == jnp.arange(experts, dtype=jnp.int32)[None, None, :]
    weights = jnp.sum(jnp.where(onehot, gate_probs[:, :, None], 0.0), axis=1).astype(jnp.bfloat16)
    live_hits = jnp.sum(jnp.where(onehot & live_slots[:, :, None], 1, 0), axis=1).astype(jnp.int32)
    local_counts = jnp.sum(live_hits, axis=0)
    offsets = carried_in(local_counts, "expert", add_counts, jnp.zeros_like(local_counts))
    running = jnp.cumsum(live_hits, axis=0) - 1 + offsets[None, :]
    token_places = jnp.where(live_hits > 0, running, -1).astype(jnp.int32)
    first_expert = lax.axis_index("expert") * local_count
    hidden = saved_hidden[0]
    capacity = hidden.shape[1]
    row_count = token_count * owners
    slot_iota = jnp.arange(capacity, dtype=jnp.int32)
    positions = jnp.full((local_count, row_count), -1, jnp.int32)
    cotangents = lax.all_gather(cotangent, "expert", axis=0, tiled=True)
    gate_rows = lax.all_gather(weights, "expert", axis=0, tiled=True)
    place_rows = lax.all_gather(token_places, "expert", axis=0, tiled=True)
    columns = lax.dynamic_slice_in_dim(gate_rows, first_expert, local_count, 1)
    places = lax.dynamic_slice_in_dim(place_rows, first_expert, local_count, 1)
    select = (places.T[:, None, :] == slot_iota[None, :, None]).astype(jnp.bfloat16)
    slot_rows = jnp.einsum(
        "ecn,nd->ecd", select, cotangents, preferred_element_type=jnp.float32
    ).astype(jnp.bfloat16)
    slot_gates = jnp.einsum("ecn,ne->ec", select, columns, preferred_element_type=jnp.float32)
    positions = lax.dynamic_update_slice_in_dim(positions, places.T, jnp.int32(0), 1)
    slot_rows, slot_gates, positions = (slot_rows, slot_gates, positions)
    wide_rows = slot_rows.astype(jnp.float32)
    scaled = (slot_gates[:, :, None] * wide_rows).astype(jnp.bfloat16)
    grad_rows = jnp.einsum("ecf,ecd->efd", hidden, scaled, preferred_element_type=jnp.float32)
    outputs = jnp.einsum("ecf,efd->ecd", hidden, down_weight, preferred_element_type=jnp.float32)
    slot_scores = jnp.sum(outputs * wide_rows, axis=-1)
    safe_places = jnp.maximum(positions, 0)
    scores = jnp.where(positions >= 0, jnp.take_along_axis(slot_scores, safe_places, axis=1), 0.0)
    returned = lax.all_to_all(
        scores.reshape(local_count, owners, token_count),
        "expert",
        split_axis=1,
        concat_axis=0,
        tiled=True,
    )
    returned = returned.reshape(experts, token_count)
    picked = jnp.sum(jnp.where(onehot, returned.T[:, None, :], 0.0), axis=2)
    average = jnp.sum(jnp.where(live_slots, picked, 0.0), axis=1) / counts.astype(jnp.float32)
    router_grad = jnp.where(live_slots, picked - average[:, None], 0.0)
    replicas = lax.axis_size("dp")
    level_count = replicas.bit_length() - 1
    shard_rows = hidden_width // replicas
    stacked = lax.all_to_all(
        grad_rows.reshape(local_count, replicas, shard_rows, model_width),
        "dp",
        split_axis=1,
        concat_axis=1,
        tiled=True,
    )
    for level_index in range(level_count):
        half_rows = stacked.shape[1] // 2
        stacked = adasum_pair(stacked[:, :half_rows], stacked[:, half_rows:])
    merged = stacked[:, 0]
    return (router_grad, merged)


MESH = pl.DeviceIdType.MESH
CHUNKS = 8
TOP = 32767.0


def flipped(position, mask):
    result = position
    bit = 1
    while bit <= mask:
        if mask & bit:
            result = result + bit * (1 - 2 * ((position // bit) % 2))
        bit *= 2
    return result


def merge_kernel(
    owners, replicas, chunks,
    gates_ref, cot_ref, hid_ref, w_ref,
    score_ref, own_ref, got, table_ref,
    cots, gate_out, gates, hid, weight, hid_t, tok_t, gate_cols, scaled, own, enc, enc_scale, got_scale, score_mine, score_back,
    load_sem, keep_sem, own_sem, gate_s, gate_r, direct_s, direct_r, forward_s, forward_r,
    grad_s, grad_r, scale_s, scale_r, back_s, back_r,
):
    me = lax.axis_index("expert")
    mine = lax.axis_index("dp")
    sibling = me + 1 - 2 * (me % 2)
    pairs = owners // 2
    tokens = cot_ref.shape[0]
    width = cot_ref.shape[1] // chunks
    local_count, capacity, hidden_width = hid.shape
    shard = hidden_width // replicas
    row_count = owners * tokens
    lanes = got_scale.shape[-1]

    barrier = pltpu.get_barrier_semaphore()
    for j in range(1, owners):
        pl.semaphore_signal(barrier, inc=1, device_id={"expert": (me + j) % owners}, device_id_type=MESH)
    for m in range(1, replicas):
        pl.semaphore_signal(barrier, inc=1, device_id={"dp": flipped(mine, m)}, device_id_type=MESH)

    load_hid = pltpu.make_async_copy(hid_ref, hid, load_sem.at[0])
    load_w = pltpu.make_async_copy(w_ref, weight, load_sem.at[1])

    def block(source):
        return pl.ds(pl.multiple_of(source * tokens, tokens), tokens)

    def columns(k):
        return pl.ds(pl.multiple_of(k * width, width), width)

    def own_copy(k):
        return pltpu.make_async_copy(cot_ref.at[:, columns(k)], cots.at[k, block(me)], own_sem.at[k])

    def gate_copy(j):
        target = (me + j) % owners
        return pltpu.make_async_remote_copy(
            gate_out.at[target], gates.at[me], gate_s.at[j - 1], gate_r.at[j - 1],
            device_id={"expert": target}, device_id_type=MESH)

    def direct_copy(j, k):
        target = sibling if j == 0 else (me + 2 * j) % owners
        return pltpu.make_async_remote_copy(
            cot_ref.at[:, columns(k)], cots.at[k, block(me)], direct_s.at[j, k], direct_r.at[j, k],
            device_id={"expert": target}, device_id_type=MESH)

    def forward_copy(j, k):
        piece = cots.at[k, block((me + owners - 2 * j) % owners)]
        return pltpu.make_async_remote_copy(
            piece, piece, forward_s.at[j - 1, k], forward_r.at[j - 1, k],
            device_id={"expert": sibling}, device_id_type=MESH)

    def grad_copy(m, k):
        return pltpu.make_async_remote_copy(
            enc.at[m - 1, k], got.at[m - 1, k], grad_s.at[m - 1, k], grad_r.at[m - 1, k],
            device_id={"dp": flipped(mine, m)}, device_id_type=MESH)

    def scale_copy(m, k):
        return pltpu.make_async_remote_copy(
            enc_scale.at[m - 1, k], got_scale.at[m - 1, k], scale_s.at[m - 1, k], scale_r.at[m - 1, k],
            device_id={"dp": flipped(mine, m)}, device_id_type=MESH)

    def back_copy(j):
        target = (me + j) % owners
        return pltpu.make_async_remote_copy(
            score_mine.at[target], score_back.at[me], back_s.at[j - 1], back_r.at[j - 1],
            device_id={"expert": target}, device_id_type=MESH)

    def keep_copy(k):
        return pltpu.make_async_copy(own.at[k], own_ref.at[k], keep_sem.at[k])

    load_hid.start()
    gate_out[...] = jnp.zeros_like(gate_out)
    for s in range(owners):
        gate_out[s, :local_count, :] = gates_ref[s * local_count:(s + 1) * local_count, :]
    pl.semaphore_wait(barrier, owners - 1 + replicas - 1)
    for j in range(1, owners):
        gate_copy(j).start()

    def send_cots(k):
        for j in range(pairs):
            direct_copy(j, k).start()

    send_cots(0)

    def start_own(k, carry):
        own_copy(k).start()
        return carry

    lax.fori_loop(0, chunks, start_own, 0)
    load_w.start()
    gates[me] = gate_out[me]
    score_mine[...] = jnp.zeros_like(score_mine)
    enc_scale[...] = jnp.zeros_like(enc_scale)

    load_hid.wait()

    def turn(b, carry):
        rows = pl.ds(pl.multiple_of(b * 128, 128), 128)
        for e in range(local_count):
            hid_t[e, :, rows] = hid[e, rows, :].astype(jnp.float32).T.astype(jnp.bfloat16)
        return carry

    lax.fori_loop(0, capacity // 128, turn, 0)

    for j in range(1, owners):
        gate_copy(j).wait_recv()

    eye = (lax.broadcasted_iota(jnp.int32, (tokens, tokens), 0)
           == lax.broadcasted_iota(jnp.int32, (tokens, tokens), 1))
    upper = (lax.broadcasted_iota(jnp.int32, (tokens, tokens), 0)
             <= lax.broadcasted_iota(jnp.int32, (tokens, tokens), 1)).astype(jnp.bfloat16)
    slots = lax.broadcasted_iota(jnp.int32, (capacity, 2 * tokens), 0)
    for e in range(local_count):
        rows = jnp.concatenate([gates[s, e:e + 1, :] for s in range(owners)], axis=0)
        hit = rows > 0.0
        inside = jnp.dot(jnp.where(hit, 1.0, 0.0).astype(jnp.bfloat16), upper, preferred_element_type=jnp.float32)
        before = jnp.zeros((1, 1), jnp.float32)
        places = []
        for s in range(owners):
            place = inside[s:s + 1, :] + before - 1.0
            places.append(jnp.where(hit[s:s + 1, :], place, -1.0).astype(jnp.int32))
            before = before + inside[s:s + 1, tokens - 1:tokens]
            column = jnp.sum(jnp.where(eye, rows[s:s + 1, :], 0.0), axis=1, keepdims=True)
            gate_cols[e, s * tokens:(s + 1) * tokens, :] = jnp.broadcast_to(column, (tokens, 128))
        for pair in range(pairs):
            place = jnp.concatenate(places[2 * pair:2 * pair + 2], axis=1)
            select = jnp.where(slots == place, 1.0, 0.0).astype(jnp.bfloat16)
            tok_t[e, :, pair * 2 * tokens:(pair + 1) * 2 * tokens] = jnp.dot(
                hid_t[e], select, preferred_element_type=jnp.float32).astype(jnp.bfloat16)

    mark = (lax.broadcasted_iota(jnp.int32, (shard, lanes), 0)
            == lax.broadcasted_iota(jnp.int32, (shard, lanes), 1))

    def step(k, carry):
        own_copy(k).wait()
        for j in range(1, pairs):
            direct_copy(j, k).wait_recv()
            forward_copy(j, k).start()
        direct_copy(0, k).wait_recv()

        @pl.when(k + 1 < chunks)
        def _():
            send_cots(k + 1)

        for j in range(1, pairs):
            forward_copy(j, k).wait_recv()

        def scale_block(s, carry):
            for e in range(local_count):
                gate = gate_cols[e, block(s), :]
                for c in range(width // 128):
                    part = cots[k, block(s), c * 128:(c + 1) * 128].astype(jnp.float32)
                    scaled[e, block(s), c * 128:(c + 1) * 128] = (gate * part).astype(jnp.bfloat16)
            return carry

        lax.fori_loop(0, owners, scale_block, 0)
        for m in list(range(replicas - 1, 0, -1)) + [0]:
            target = flipped(mine, m)
            rows = pl.ds(pl.multiple_of(target * shard, shard), shard)
            for e in range(local_count):
                grad = jnp.dot(tok_t[e, rows, :], scaled[e], preferred_element_type=jnp.float32)
                if m == 0:
                    own[k, e] = grad
                else:
                    largest = jnp.max(jnp.abs(grad), axis=1, keepdims=True)
                    factor = jnp.where(largest > 1e-30, TOP / largest, 0.0)
                    enc[m - 1, k, e] = jnp.round(grad * factor).astype(jnp.int32).astype(jnp.int16)
                    enc_scale[m - 1, k, e:e + 1, :] = jnp.sum(
                        jnp.where(mark, largest * (1.0 / TOP), 0.0), axis=0, keepdims=True)
            if m:
                scale_copy(m, k).start()
                grad_copy(m, k).start()
            else:
                keep_copy(k).start()
        return carry

    lax.fori_loop(0, chunks, step, 0)

    load_w.wait()
    half = hidden_width // 256

    def score_pair(pair, carry):
        toks = pl.ds(pl.multiple_of(pair * 2 * tokens, 2 * tokens), 2 * tokens)
        for e in range(local_count):
            total = jnp.zeros((1, 2 * tokens), jnp.float32)
            for f in range(half):
                part = jnp.zeros((256, 2 * tokens), jnp.float32)
                for k in range(chunks):
                    part = part + lax.dot_general(
                        weight[e, f * 256:(f + 1) * 256, k * width:(k + 1) * width], cots[k, toks, :],
                        (((1,), (1,)), ((), ())), preferred_element_type=jnp.float32)
                total = total + jnp.sum(
                    part * tok_t[e, f * 256:(f + 1) * 256, toks].astype(jnp.float32), axis=0, keepdims=True)
            score_mine[2 * pair, e:e + 1, :] = total[:, :tokens]
            score_mine[2 * pair + 1, e:e + 1, :] = total[:, tokens:]
        return carry

    lax.fori_loop(0, pairs, score_pair, 0)
    for j in range(1, owners):
        back_copy(j).start()
    score_back[me] = score_mine[me]

    for k in range(chunks):
        for m in range(1, replicas):
            scale_copy(m, k).wait_recv()
    for e in range(local_count):
        rows = [got_scale[m, k, e:e + 1, :] for m in range(replicas - 1) for k in range(chunks)]
        rows.append(jnp.zeros((128 - len(rows), lanes), jnp.float32))
        table_ref[e] = jnp.concatenate(rows, axis=0).T[:shard]

    for j in range(1, owners):
        back_copy(j).wait_recv()
    for s in range(owners):
        score_ref[s * local_count:(s + 1) * local_count, :] = score_back[s, :local_count, :]
    for k in range(chunks):
        keep_copy(k).wait()
        for m in range(1, replicas):
            grad_copy(m, k).wait_recv()

    for j in range(1, owners):
        gate_copy(j).wait_send()
        back_copy(j).wait_send()

    def drain(k, carry):
        for j in range(pairs):
            direct_copy(j, k).wait_send()
            if j:
                forward_copy(j, k).wait_send()
        for m in range(1, replicas):
            scale_copy(m, k).wait_send()
            grad_copy(m, k).wait_send()
        return carry

    lax.fori_loop(0, chunks, drain, 0)


def adasum_kernel(own_ref, got_ref, table_ref, out_ref):
    others, chunks = got_ref.shape[:2]
    width = got_ref.shape[-1]

    def dots(left, right):
        return jnp.sum(sum(a * b for a, b in zip(left, right)), axis=1, keepdims=True)

    def merge_rows(b, carry):
        rows = pl.ds(pl.multiple_of(b * 16, 16), 16)
        scales = table_ref[0, rows, :]
        grads = [[own_ref[k, 0, rows, :] for k in range(chunks)]]
        for m in range(others):
            parts = []
            for k in range(chunks):
                at = m * chunks + k
                parts.append(got_ref[m, k, 0, rows, :].astype(jnp.int32).astype(jnp.float32) * scales[:, at:at + 1])
            grads.append(parts)
        while len(grads) > 1:
            count = len(grads) // 2
            merged = []
            for left, right in zip(grads[:count], grads[count:]):
                inner = dots(left, right)
                left_coef = 1.0 - inner / (2.0 * (dots(left, left) + epsilon))
                right_coef = 1.0 - inner / (2.0 * (dots(right, right) + epsilon))
                merged.append([left_coef * a + right_coef * b for a, b in zip(left, right)])
            grads = merged
        for k in range(chunks):
            out_ref[0, rows, k * width:(k + 1) * width] = grads[0][k]
        return carry

    lax.fori_loop(0, out_ref.shape[1] // 16, merge_rows, 0, unroll=True)


def fused(owners, replicas, route_ids, counts, slot_probs, cotangent, saved_hidden, down_weight):
    tokens, model_width = cotangent.shape
    slot_count = route_ids.shape[1]
    local_count, hidden_width = down_weight.shape[:2]
    capacity = saved_hidden.shape[2]
    experts = local_count * owners
    chunks = CHUNKS
    width = model_width // chunks
    shard = hidden_width // replicas
    lanes = -(-shard // 128) * 128
    others = replicas - 1
    pairs = owners // 2
    live_slots = jnp.arange(slot_count, dtype=jnp.int32)[None, :] < counts[:, None]
    onehot = route_ids[:, :, None] == jnp.arange(experts, dtype=jnp.int32)[None, None, :]
    gate_probs = jnp.where(live_slots, slot_probs.astype(jnp.float32), 0.0)
    weights = jnp.sum(jnp.where(onehot, gate_probs[:, :, None], 0.0), axis=1)
    gates = weights.T
    f32, bf16, i16 = jnp.float32, jnp.bfloat16, jnp.int16
    dma = pltpu.SemaphoreType.DMA
    vmem = pl.BlockSpec(memory_space=pltpu.VMEM)
    anywhere = pl.BlockSpec(memory_space=pl.ANY)
    returned, own, got, table = pl.pallas_call(
        functools.partial(merge_kernel, owners, replicas, chunks),
        out_shape=(
            jax.ShapeDtypeStruct((experts, tokens), f32),
            jax.ShapeDtypeStruct((chunks, local_count, shard, width), f32),
            jax.ShapeDtypeStruct((others, chunks, local_count, shard, width), i16),
            jax.ShapeDtypeStruct((local_count, shard, 128), f32),
        ),
        in_specs=[vmem, anywhere, anywhere, anywhere],
        out_specs=(vmem, anywhere, anywhere, vmem),
        scratch_shapes=[
            pltpu.VMEM((chunks, owners * tokens, width), bf16),
            pltpu.VMEM((owners, 8, tokens), f32),
            pltpu.VMEM((owners, 8, tokens), f32),
            pltpu.VMEM((local_count, capacity, hidden_width), bf16),
            pltpu.VMEM((local_count, hidden_width, model_width), bf16),
            pltpu.VMEM((local_count, hidden_width, capacity), bf16),
            pltpu.VMEM((local_count, hidden_width, owners * tokens), bf16),
            pltpu.VMEM((local_count, owners * tokens, 128), f32),
            pltpu.VMEM((local_count, owners * tokens, width), bf16),
            pltpu.VMEM((chunks, local_count, shard, width), f32),
            pltpu.VMEM((others, chunks, local_count, shard, width), i16),
            pltpu.VMEM((others, chunks, 8, lanes), f32),
            pltpu.VMEM((others, chunks, 8, lanes), f32),
            pltpu.VMEM((owners, 8, tokens), f32),
            pltpu.VMEM((owners, 8, tokens), f32),
            dma((2,)), dma((chunks,)), dma((chunks,)),
            dma((owners - 1,)), dma((owners - 1,)),
            dma((pairs, chunks)), dma((pairs, chunks)),
            dma((pairs - 1, chunks)), dma((pairs - 1, chunks)),
            dma((others, chunks)), dma((others, chunks)),
            dma((others, chunks)), dma((others, chunks)),
            dma((owners - 1,)), dma((owners - 1,)),
        ],
        compiler_params=pltpu.CompilerParams(
            collective_id=0, has_side_effects=True, vmem_limit_bytes=56 * 2**20),
    )(gates, cotangent, saved_hidden[0], down_weight)
    rows = 96 if shard % 96 == 0 else 16
    merged = pl.pallas_call(
        adasum_kernel,
        grid=(local_count, shard // rows),
        out_shape=jax.ShapeDtypeStruct((local_count, shard, model_width), f32),
        in_specs=[
            pl.BlockSpec((chunks, 1, rows, width), lambda e, b: (0, e, b, 0)),
            pl.BlockSpec((others, chunks, 1, rows, width), lambda e, b: (0, 0, e, b, 0)),
            pl.BlockSpec((1, rows, 128), lambda e, b: (e, b, 0)),
        ],
        out_specs=pl.BlockSpec((1, rows, model_width), lambda e, b: (e, b, 0)),
        compiler_params=pltpu.CompilerParams(vmem_limit_bytes=60 * 2**20),
    )(own, got, table)
    picked = jnp.sum(jnp.where(onehot, returned.T[:, None, :], 0.0), axis=2)
    average = jnp.sum(jnp.where(live_slots, picked, 0.0), axis=1) / counts.astype(jnp.float32)
    router_grad = jnp.where(live_slots, picked - average[:, None], 0.0)
    return (router_grad, merged)


def chosen(owners, replicas, *arrays):
    cotangent, saved_hidden, down_weight = arrays[3:]
    local_count, hidden_width, model_width = down_weight.shape
    shard = hidden_width // replicas
    fits = (
        owners >= 4 and owners % 2 == 0 and local_count <= 8
        and replicas >= 2 and (replicas - 1) * CHUNKS < 128 and replicas & (replicas - 1) == 0 and shard % 16 == 0
        and hidden_width % 256 == 0 and model_width % (128 * CHUNKS) == 0
        and saved_hidden.shape[2] % 128 == 0 and cotangent.shape[0] == 128
    )
    return fused(owners, replicas, *arrays) if fits else local(*arrays)


def solution(mesh):
    in_specs = (
        P(("dp", "expert"), None),
        P(("dp", "expert")),
        P(("dp", "expert"), None),
        P(("dp", "expert"), None),
        P("dp", "expert", None, None),
        P("expert", None, None),
    )
    out_specs = (P(("dp", "expert"), None), P("expert", "dp", None))
    body = functools.partial(chosen, mesh.shape["expert"], mesh.shape["dp"])
    return jax.shard_map(body, mesh=mesh, in_specs=in_specs, out_specs=out_specs, check_vma=False)
```

```python
import functools

import jax
import jax.numpy as jnp
from jax import lax
from jax.experimental import pallas as pl
from jax.experimental.pallas import tpu as pltpu
from jax.sharding import PartitionSpec as P

epsilon = 1e-06


def carried_in(value, axis, join, neutral):
    count, mine = (lax.axis_size(axis), lax.axis_index(axis))
    pieces = lax.all_gather(value, axis)
    running = jnp.full_like(value, 0) + jnp.asarray(neutral, value.dtype)

    def lap(position, running):
        longer = join(running, pieces[position])
        return jnp.where(position < mine, longer, running)

    return lax.fori_loop(0, count - 1, lap, running)


def adasum_pair(left_grad, right_grad):
    inner = jnp.sum(left_grad * right_grad, axis=-1, keepdims=True)
    left_norm = jnp.sum(left_grad * left_grad, axis=-1, keepdims=True)
    right_norm = jnp.sum(right_grad * right_grad, axis=-1, keepdims=True)
    left_coef = 1.0 - inner / (2.0 * (left_norm + epsilon))
    right_coef = 1.0 - inner / (2.0 * (right_norm + epsilon))
    return left_coef * left_grad + right_coef * right_grad


def add_counts(earlier, later):
    return earlier + later


def local(route_ids, counts, slot_probs, cotangent, saved_hidden, down_weight):
    token_count = cotangent.shape[0]
    model_width = cotangent.shape[1]
    slot_count = route_ids.shape[1]
    owners = lax.axis_size("expert")
    local_count = down_weight.shape[0]
    hidden_width = down_weight.shape[1]
    experts = local_count * owners
    slot_index = jnp.arange(slot_count, dtype=jnp.int32)
    live_slots = slot_index[None, :] < counts[:, None]
    gate_probs = jnp.where(live_slots, slot_probs.astype(jnp.float32), 0.0)
    onehot = route_ids[:, :, None] == jnp.arange(experts, dtype=jnp.int32)[None, None, :]
    weights = jnp.sum(jnp.where(onehot, gate_probs[:, :, None], 0.0), axis=1).astype(jnp.bfloat16)
    live_hits = jnp.sum(jnp.where(onehot & live_slots[:, :, None], 1, 0), axis=1).astype(jnp.int32)
    local_counts = jnp.sum(live_hits, axis=0)
    offsets = carried_in(local_counts, "expert", add_counts, jnp.zeros_like(local_counts))
    running = jnp.cumsum(live_hits, axis=0) - 1 + offsets[None, :]
    token_places = jnp.where(live_hits > 0, running, -1).astype(jnp.int32)
    first_expert = lax.axis_index("expert") * local_count
    hidden = saved_hidden[0]
    capacity = hidden.shape[1]
    row_count = token_count * owners
    slot_iota = jnp.arange(capacity, dtype=jnp.int32)
    positions = jnp.full((local_count, row_count), -1, jnp.int32)
    cotangents = lax.all_gather(cotangent, "expert", axis=0, tiled=True)
    gate_rows = lax.all_gather(weights, "expert", axis=0, tiled=True)
    place_rows = lax.all_gather(token_places, "expert", axis=0, tiled=True)
    columns = lax.dynamic_slice_in_dim(gate_rows, first_expert, local_count, 1)
    places = lax.dynamic_slice_in_dim(place_rows, first_expert, local_count, 1)
    select = (places.T[:, None, :] == slot_iota[None, :, None]).astype(jnp.bfloat16)
    slot_rows = jnp.einsum(
        "ecn,nd->ecd", select, cotangents, preferred_element_type=jnp.float32
    ).astype(jnp.bfloat16)
    slot_gates = jnp.einsum("ecn,ne->ec", select, columns, preferred_element_type=jnp.float32)
    positions = lax.dynamic_update_slice_in_dim(positions, places.T, jnp.int32(0), 1)
    slot_rows, slot_gates, positions = (slot_rows, slot_gates, positions)
    wide_rows = slot_rows.astype(jnp.float32)
    scaled = (slot_gates[:, :, None] * wide_rows).astype(jnp.bfloat16)
    grad_rows = jnp.einsum("ecf,ecd->efd", hidden, scaled, preferred_element_type=jnp.float32)
    outputs = jnp.einsum("ecf,efd->ecd", hidden, down_weight, preferred_element_type=jnp.float32)
    slot_scores = jnp.sum(outputs * wide_rows, axis=-1)
    safe_places = jnp.maximum(positions, 0)
    scores = jnp.where(positions >= 0, jnp.take_along_axis(slot_scores, safe_places, axis=1), 0.0)
    returned = lax.all_to_all(
        scores.reshape(local_count, owners, token_count),
        "expert",
        split_axis=1,
        concat_axis=0,
        tiled=True,
    )
    returned = returned.reshape(experts, token_count)
    picked = jnp.sum(jnp.where(onehot, returned.T[:, None, :], 0.0), axis=2)
    average = jnp.sum(jnp.where(live_slots, picked, 0.0), axis=1) / counts.astype(jnp.float32)
    router_grad = jnp.where(live_slots, picked - average[:, None], 0.0)
    replicas = lax.axis_size("dp")
    level_count = replicas.bit_length() - 1
    shard_rows = hidden_width // replicas
    stacked = lax.all_to_all(
        grad_rows.reshape(local_count, replicas, shard_rows, model_width),
        "dp",
        split_axis=1,
        concat_axis=1,
        tiled=True,
    )
    for level_index in range(level_count):
        half_rows = stacked.shape[1] // 2
        stacked = adasum_pair(stacked[:, :half_rows], stacked[:, half_rows:])
    merged = stacked[:, 0]
    return (router_grad, merged)


MESH = pl.DeviceIdType.MESH
CHUNKS = 8
TOP = 32767.0


def flipped(position, mask):
    result = position
    bit = 1
    while bit <= mask:
        if mask & bit:
            result = result + bit * (1 - 2 * ((position // bit) % 2))
        bit *= 2
    return result


def merge_kernel(
    owners, replicas, chunks,
    gates_ref, cot_ref, hid_ref, w_ref,
    score_ref, own_ref, got, table_ref,
    cots, gate_out, gates, hid, weight, hid_t, tok_t, gate_cols, scaled, own, enc, enc_scale, got_scale, score_mine, score_back,
    load_sem, keep_sem, own_sem, gate_s, gate_r, direct_s, direct_r, forward_s, forward_r,
    grad_s, grad_r, scale_s, scale_r, back_s, back_r,
):
    me = lax.axis_index("expert")
    mine = lax.axis_index("dp")
    sibling = me + 1 - 2 * (me % 2)
    pairs = owners // 2
    tokens = cot_ref.shape[0]
    width = cot_ref.shape[1] // chunks
    local_count, capacity, hidden_width = hid.shape
    shard = hidden_width // replicas
    row_count = owners * tokens
    lanes = got_scale.shape[-1]

    barrier = pltpu.get_barrier_semaphore()
    for j in range(1, owners):
        pl.semaphore_signal(barrier, inc=1, device_id={"expert": (me + j) % owners}, device_id_type=MESH)
    for m in range(1, replicas):
        pl.semaphore_signal(barrier, inc=1, device_id={"dp": flipped(mine, m)}, device_id_type=MESH)

    load_hid = pltpu.make_async_copy(hid_ref, hid, load_sem.at[0])
    load_w = pltpu.make_async_copy(w_ref, weight, load_sem.at[1])

    def block(source):
        return pl.ds(pl.multiple_of(source * tokens, tokens), tokens)

    def columns(k):
        return pl.ds(pl.multiple_of(k * width, width), width)

    def own_copy(k):
        return pltpu.make_async_copy(cot_ref.at[:, columns(k)], cots.at[k, block(me)], own_sem.at[k])

    def gate_copy(j):
        target = (me + j) % owners
        return pltpu.make_async_remote_copy(
            gate_out.at[target], gates.at[me], gate_s.at[j - 1], gate_r.at[j - 1],
            device_id={"expert": target}, device_id_type=MESH)

    def direct_copy(j, k):
        target = sibling if j == 0 else (me + 2 * j) % owners
        return pltpu.make_async_remote_copy(
            cot_ref.at[:, columns(k)], cots.at[k, block(me)], direct_s.at[j, k], direct_r.at[j, k],
            device_id={"expert": target}, device_id_type=MESH)

    def forward_copy(j, k):
        piece = cots.at[k, block((me + owners - 2 * j) % owners)]
        return pltpu.make_async_remote_copy(
            piece, piece, forward_s.at[j - 1, k], forward_r.at[j - 1, k],
            device_id={"expert": sibling}, device_id_type=MESH)

    def grad_copy(m, k):
        return pltpu.make_async_remote_copy(
            enc.at[m - 1, k], got.at[m - 1, k], grad_s.at[m - 1, k], grad_r.at[m - 1, k],
            device_id={"dp": flipped(mine, m)}, device_id_type=MESH)

    def scale_copy(m, k):
        return pltpu.make_async_remote_copy(
            enc_scale.at[m - 1, k], got_scale.at[m - 1, k], scale_s.at[m - 1, k], scale_r.at[m - 1, k],
            device_id={"dp": flipped(mine, m)}, device_id_type=MESH)

    def back_copy(j):
        target = (me + j) % owners
        return pltpu.make_async_remote_copy(
            score_mine.at[target], score_back.at[me], back_s.at[j - 1], back_r.at[j - 1],
            device_id={"expert": target}, device_id_type=MESH)

    def keep_copy(k):
        return pltpu.make_async_copy(own.at[k], own_ref.at[k], keep_sem.at[k])

    load_hid.start()
    gate_out[...] = jnp.zeros_like(gate_out)
    for s in range(owners):
        gate_out[s, :local_count, :] = gates_ref[s * local_count:(s + 1) * local_count, :]
    pl.semaphore_wait(barrier, owners - 1 + replicas - 1)
    for j in range(1, owners):
        gate_copy(j).start()

    def send_cots(k):
        for j in range(pairs):
            direct_copy(j, k).start()

    send_cots(0)

    def start_own(k, carry):
        own_copy(k).start()
        return carry

    lax.fori_loop(0, chunks, start_own, 0)
    gates[me] = gate_out[me]
    score_mine[...] = jnp.zeros_like(score_mine)
    enc_scale[...] = jnp.zeros_like(enc_scale)

    load_hid.wait()

    def turn(b, carry):
        rows = pl.ds(pl.multiple_of(b * 128, 128), 128)
        for e in range(local_count):
            hid_t[e, :, rows] = hid[e, rows, :].astype(jnp.float32).T.astype(jnp.bfloat16)
        return carry

    lax.fori_loop(0, capacity // 128, turn, 0)

    for j in range(1, owners):
        gate_copy(j).wait_recv()

    eye = (lax.broadcasted_iota(jnp.int32, (tokens, tokens), 0)
           == lax.broadcasted_iota(jnp.int32, (tokens, tokens), 1))
    upper = (lax.broadcasted_iota(jnp.int32, (tokens, tokens), 0)
             <= lax.broadcasted_iota(jnp.int32, (tokens, tokens), 1)).astype(jnp.bfloat16)
    slots = lax.broadcasted_iota(jnp.int32, (capacity, 2 * tokens), 0)
    for e in range(local_count):
        rows = jnp.concatenate([gates[s, e:e + 1, :] for s in range(owners)], axis=0)
        hit = rows > 0.0
        inside = jnp.dot(jnp.where(hit, 1.0, 0.0).astype(jnp.bfloat16), upper, preferred_element_type=jnp.float32)
        before = jnp.zeros((1, 1), jnp.float32)
        places = []
        for s in range(owners):
            place = inside[s:s + 1, :] + before - 1.0
            places.append(jnp.where(hit[s:s + 1, :], place, -1.0).astype(jnp.int32))
            before = before + inside[s:s + 1, tokens - 1:tokens]
            column = jnp.sum(jnp.where(eye, rows[s:s + 1, :], 0.0), axis=1, keepdims=True)
            gate_cols[e, s * tokens:(s + 1) * tokens, :] = jnp.broadcast_to(column, (tokens, 128))
        for pair in range(pairs):
            place = jnp.concatenate(places[2 * pair:2 * pair + 2], axis=1)
            select = jnp.where(slots == place, 1.0, 0.0).astype(jnp.bfloat16)
            tok_t[e, :, pair * 2 * tokens:(pair + 1) * 2 * tokens] = jnp.dot(
                hid_t[e], select, preferred_element_type=jnp.float32).astype(jnp.bfloat16)

    mark = (lax.broadcasted_iota(jnp.int32, (shard, lanes), 0)
            == lax.broadcasted_iota(jnp.int32, (shard, lanes), 1))

    def step(k, carry):
        own_copy(k).wait()
        for j in range(1, pairs):
            direct_copy(j, k).wait_recv()
            forward_copy(j, k).start()
        direct_copy(0, k).wait_recv()

        @pl.when(k + 1 < chunks)
        def _():
            send_cots(k + 1)

        for j in range(1, pairs):
            forward_copy(j, k).wait_recv()

        def scale_block(s, carry):
            for e in range(local_count):
                gate = gate_cols[e, block(s), :]
                for c in range(width // 128):
                    part = cots[k, block(s), c * 128:(c + 1) * 128].astype(jnp.float32)
                    scaled[e, block(s), c * 128:(c + 1) * 128] = (gate * part).astype(jnp.bfloat16)
            return carry

        lax.fori_loop(0, owners, scale_block, 0)
        for m in list(range(replicas - 1, 0, -1)) + [0]:
            target = flipped(mine, m)
            rows = pl.ds(pl.multiple_of(target * shard, shard), shard)
            for e in range(local_count):
                grad = jnp.dot(tok_t[e, rows, :], scaled[e], preferred_element_type=jnp.float32)
                if m == 0:
                    own[k, e] = grad
                else:
                    largest = jnp.max(jnp.abs(grad), axis=1, keepdims=True)
                    factor = jnp.where(largest > 1e-30, TOP / largest, 0.0)
                    enc[m - 1, k, e] = jnp.round(grad * factor).astype(jnp.int32).astype(jnp.int16)
                    enc_scale[m - 1, k, e:e + 1, :] = jnp.sum(
                        jnp.where(mark, largest * (1.0 / TOP), 0.0), axis=0, keepdims=True)
            if m:
                scale_copy(m, k).start()
                grad_copy(m, k).start()
            else:
                keep_copy(k).start()
        return carry

    load_w.start()
    lax.fori_loop(0, chunks, step, 0)

    load_w.wait()
    half = hidden_width // 256

    def score_pair(pair, carry):
        toks = pl.ds(pl.multiple_of(pair * 2 * tokens, 2 * tokens), 2 * tokens)
        for e in range(local_count):
            total = jnp.zeros((1, 2 * tokens), jnp.float32)
            for f in range(half):
                part = jnp.zeros((256, 2 * tokens), jnp.float32)
                for k in range(chunks):
                    part = part + lax.dot_general(
                        weight[e, f * 256:(f + 1) * 256, k * width:(k + 1) * width], cots[k, toks, :],
                        (((1,), (1,)), ((), ())), preferred_element_type=jnp.float32)
                total = total + jnp.sum(
                    part * tok_t[e, f * 256:(f + 1) * 256, toks].astype(jnp.float32), axis=0, keepdims=True)
            score_mine[2 * pair, e:e + 1, :] = total[:, :tokens]
            score_mine[2 * pair + 1, e:e + 1, :] = total[:, tokens:]
        return carry

    lax.fori_loop(0, pairs, score_pair, 0)
    for j in range(1, owners):
        back_copy(j).start()
    score_back[me] = score_mine[me]

    for k in range(chunks):
        for m in range(1, replicas):
            scale_copy(m, k).wait_recv()
    for e in range(local_count):
        rows = [got_scale[m, k, e:e + 1, :] for m in range(replicas - 1) for k in range(chunks)]
        rows.append(jnp.zeros((128 - len(rows), lanes), jnp.float32))
        table_ref[e] = jnp.concatenate(rows, axis=0).T[:shard]

    for j in range(1, owners):
        back_copy(j).wait_recv()
    for s in range(owners):
        score_ref[s * local_count:(s + 1) * local_count, :] = score_back[s, :local_count, :]
    for k in range(chunks):
        keep_copy(k).wait()
        for m in range(1, replicas):
            grad_copy(m, k).wait_recv()

    for j in range(1, owners):
        gate_copy(j).wait_send()
        back_copy(j).wait_send()

    def drain(k, carry):
        for j in range(pairs):
            direct_copy(j, k).wait_send()
            if j:
                forward_copy(j, k).wait_send()
        for m in range(1, replicas):
            scale_copy(m, k).wait_send()
            grad_copy(m, k).wait_send()
        return carry

    lax.fori_loop(0, chunks, drain, 0)


def adasum_kernel(own_ref, got_ref, table_ref, out_ref):
    others, chunks = got_ref.shape[:2]
    width = got_ref.shape[-1]

    def dots(left, right):
        return jnp.sum(sum(a * b for a, b in zip(left, right)), axis=1, keepdims=True)

    def merge_rows(b, carry):
        rows = pl.ds(pl.multiple_of(b * 16, 16), 16)
        scales = table_ref[0, rows, :]
        grads = [[own_ref[k, 0, rows, :] for k in range(chunks)]]
        for m in range(others):
            parts = []
            for k in range(chunks):
                at = m * chunks + k
                parts.append(got_ref[m, k, 0, rows, :].astype(jnp.int32).astype(jnp.float32) * scales[:, at:at + 1])
            grads.append(parts)
        while len(grads) > 1:
            count = len(grads) // 2
            merged = []
            for left, right in zip(grads[:count], grads[count:]):
                inner = dots(left, right)
                left_coef = 1.0 - inner / (2.0 * (dots(left, left) + epsilon))
                right_coef = 1.0 - inner / (2.0 * (dots(right, right) + epsilon))
                merged.append([left_coef * a + right_coef * b for a, b in zip(left, right)])
            grads = merged
        for k in range(chunks):
            out_ref[0, rows, k * width:(k + 1) * width] = grads[0][k]
        return carry

    lax.fori_loop(0, out_ref.shape[1] // 16, merge_rows, 0, unroll=True)


def fused(owners, replicas, route_ids, counts, slot_probs, cotangent, saved_hidden, down_weight):
    tokens, model_width = cotangent.shape
    slot_count = route_ids.shape[1]
    local_count, hidden_width = down_weight.shape[:2]
    capacity = saved_hidden.shape[2]
    experts = local_count * owners
    chunks = CHUNKS
    width = model_width // chunks
    shard = hidden_width // replicas
    lanes = -(-shard // 128) * 128
    others = replicas - 1
    pairs = owners // 2
    live_slots = jnp.arange(slot_count, dtype=jnp.int32)[None, :] < counts[:, None]
    onehot = route_ids[:, :, None] == jnp.arange(experts, dtype=jnp.int32)[None, None, :]
    gate_probs = jnp.where(live_slots, slot_probs.astype(jnp.float32), 0.0)
    weights = jnp.sum(jnp.where(onehot, gate_probs[:, :, None], 0.0), axis=1)
    gates = weights.T
    f32, bf16, i16 = jnp.float32, jnp.bfloat16, jnp.int16
    dma = pltpu.SemaphoreType.DMA
    vmem = pl.BlockSpec(memory_space=pltpu.VMEM)
    anywhere = pl.BlockSpec(memory_space=pl.ANY)
    returned, own, got, table = pl.pallas_call(
        functools.partial(merge_kernel, owners, replicas, chunks),
        out_shape=(
            jax.ShapeDtypeStruct((experts, tokens), f32),
            jax.ShapeDtypeStruct((chunks, local_count, shard, width), f32),
            jax.ShapeDtypeStruct((others, chunks, local_count, shard, width), i16),
            jax.ShapeDtypeStruct((local_count, shard, 128), f32),
        ),
        in_specs=[vmem, anywhere, anywhere, anywhere],
        out_specs=(vmem, anywhere, anywhere, vmem),
        scratch_shapes=[
            pltpu.VMEM((chunks, owners * tokens, width), bf16),
            pltpu.VMEM((owners, 8, tokens), f32),
            pltpu.VMEM((owners, 8, tokens), f32),
            pltpu.VMEM((local_count, capacity, hidden_width), bf16),
            pltpu.VMEM((local_count, hidden_width, model_width), bf16),
            pltpu.VMEM((local_count, hidden_width, capacity), bf16),
            pltpu.VMEM((local_count, hidden_width, owners * tokens), bf16),
            pltpu.VMEM((local_count, owners * tokens, 128), f32),
            pltpu.VMEM((local_count, owners * tokens, width), bf16),
            pltpu.VMEM((chunks, local_count, shard, width), f32),
            pltpu.VMEM((others, chunks, local_count, shard, width), i16),
            pltpu.VMEM((others, chunks, 8, lanes), f32),
            pltpu.VMEM((others, chunks, 8, lanes), f32),
            pltpu.VMEM((owners, 8, tokens), f32),
            pltpu.VMEM((owners, 8, tokens), f32),
            dma((2,)), dma((chunks,)), dma((chunks,)),
            dma((owners - 1,)), dma((owners - 1,)),
            dma((pairs, chunks)), dma((pairs, chunks)),
            dma((pairs - 1, chunks)), dma((pairs - 1, chunks)),
            dma((others, chunks)), dma((others, chunks)),
            dma((others, chunks)), dma((others, chunks)),
            dma((owners - 1,)), dma((owners - 1,)),
        ],
        compiler_params=pltpu.CompilerParams(
            collective_id=0, has_side_effects=True, vmem_limit_bytes=56 * 2**20),
    )(gates, cotangent, saved_hidden[0], down_weight)
    rows = 96 if shard % 96 == 0 else 16
    merged = pl.pallas_call(
        adasum_kernel,
        grid=(local_count, shard // rows),
        out_shape=jax.ShapeDtypeStruct((local_count, shard, model_width), f32),
        in_specs=[
            pl.BlockSpec((chunks, 1, rows, width), lambda e, b: (0, e, b, 0)),
            pl.BlockSpec((others, chunks, 1, rows, width), lambda e, b: (0, 0, e, b, 0)),
            pl.BlockSpec((1, rows, 128), lambda e, b: (e, b, 0)),
        ],
        out_specs=pl.BlockSpec((1, rows, model_width), lambda e, b: (e, b, 0)),
        compiler_params=pltpu.CompilerParams(vmem_limit_bytes=60 * 2**20),
    )(own, got, table)
    picked = jnp.sum(jnp.where(onehot, returned.T[:, None, :], 0.0), axis=2)
    average = jnp.sum(jnp.where(live_slots, picked, 0.0), axis=1) / counts.astype(jnp.float32)
    router_grad = jnp.where(live_slots, picked - average[:, None], 0.0)
    return (router_grad, merged)


def chosen(owners, replicas, *arrays):
    cotangent, saved_hidden, down_weight = arrays[3:]
    local_count, hidden_width, model_width = down_weight.shape
    shard = hidden_width // replicas
    fits = (
        owners >= 4 and owners % 2 == 0 and local_count <= 8
        and replicas >= 2 and (replicas - 1) * CHUNKS < 128 and replicas & (replicas - 1) == 0 and shard % 16 == 0
        and hidden_width % 256 == 0 and model_width % (128 * CHUNKS) == 0
        and saved_hidden.shape[2] % 128 == 0 and cotangent.shape[0] == 128
    )
    return fused(owners, replicas, *arrays) if fits else local(*arrays)


def solution(mesh):
    in_specs = (
        P(("dp", "expert"), None),
        P(("dp", "expert")),
        P(("dp", "expert"), None),
        P(("dp", "expert"), None),
        P("dp", "expert", None, None),
        P("expert", None, None),
    )
    out_specs = (P(("dp", "expert"), None), P("expert", "dp", None))
    body = functools.partial(chosen, mesh.shape["expert"], mesh.shape["dp"])
    return jax.shard_map(body, mesh=mesh, in_specs=in_specs, out_specs=out_specs, check_vma=False)
```
